512 devices in a mesh: space: 64 (over y_lo, z, core), samp: 8 (over x, y_hi).
Axes of the slice: x: 4, y: 8 (y_hi: 2, y_lo: 4; y = y_hi * 4 + y_lo), z: 8, core: 2. Of those that a mesh axis runs over, the one named last changes fastest.
Arguments:
- snapshots: float32 [4, 512, 131072], P(None, 'samp', 'space'), may hold values from -24 to 24
- space_basis: float32 [256, 131072], P('samp', 'space'), may hold values from -0.016572815 to 0.016572815
- sample_basis: float32 [512, 64], P('samp'), may hold values from -0.26516504 to 0.26516504
Outputs:
- deflated: float32 [4, 512, 131072], P(None, 'samp', 'space')
The draws below stay inside these ranges and needn't reach their ends.
All inputs are finite; a program needn't handle non-finite values.
Results may differ from the reference program's by a relative error of at most 0.000078.
Values sent between devices are 32-bit elements; how exact they have to be, the bound alone decides.
A program may use at most 64 MiB of HBM per device.

```python
import math
import jax
import jax.numpy as jnp
from jax import lax

SAMPLES = 512
RANK_SPACE = 256
RANK_SAMP = 64
SNAPS = 4
SPACE = 131072


def common_factors(key):
    base_key = jax.random.fold_in(key, 101)
    key_space, key_sample, key_amplitude, key_noise = jax.random.split(base_key, 4)
    space_factor = jax.random.truncated_normal(key_space, -6.0, 6.0, (RANK_SPACE, SPACE), jnp.float32) / math.sqrt(SPACE)
    sample_factor = jax.random.truncated_normal(key_sample, -6.0, 6.0, (SAMPLES, RANK_SAMP), jnp.float32) / math.sqrt(SAMPLES)
    amplitudes = jax.random.normal(key_amplitude, (SNAPS, RANK_SPACE, RANK_SAMP), jnp.float32)
    amplitudes = amplitudes * (0.8 * math.sqrt(SPACE * SAMPLES / (RANK_SPACE * RANK_SAMP)))
    return (space_factor, sample_factor, amplitudes, key_noise)


def draw_space_basis(key, part):
    return common_factors(key)[0]


def draw_sample_basis(key, part):
    return common_factors(key)[1]


def draw_snapshots(key, part):
    space_factor, sample_factor, amplitudes, key_noise = common_factors(key)
    highest = lax.Precision.HIGHEST
    spread = jnp.einsum('trq,sq->trs', amplitudes, sample_factor, precision=highest)
    signal = jnp.einsum('trs,rm->tsm', spread, space_factor, precision=highest)
    independent = jax.random.normal(key_noise, (SNAPS, SAMPLES, SPACE), jnp.float32)
    return jnp.clip(signal + independent, -24.0, 24.0)


def setup_inputs(seed: int = 0) -> dict:
    key_of = jax.random.split(jax.random.key(seed), 4)
    return {
        "snapshots": draw_snapshots(jax.random.fold_in(key_of[3], 71), 0),
        "space_basis": draw_space_basis(jax.random.fold_in(key_of[3], 71), 0),
        "sample_basis": draw_sample_basis(jax.random.fold_in(key_of[3], 71), 0),
    }


def reference(snapshots, space_basis, sample_basis):
    highest = lax.Precision.HIGHEST
    contracted = jnp.einsum("rm,tsm->rts", space_basis, snapshots, precision=highest)
    core_full = jnp.einsum("rts,sq->rtq", contracted, sample_basis, precision=highest)
    spread = jnp.einsum("rtq,sq->rts", core_full, sample_basis, precision=highest)
    removed = jnp.einsum("rts,rm->tsm", spread, space_basis, precision=highest)
    return snapshots - removed
```

```python
import jax
import jax.numpy as jnp
from jax import lax
from jax.experimental import pallas as pl
from jax.experimental.pallas import tpu as pltpu
from jax.sharding import PartitionSpec as P

MESH = pl.DeviceIdType.MESH
f32, bf16 = jnp.float32, jnp.bfloat16
XS, YS, ZS, CORES = 4, 8, 8, 2
CHUNKS = 4
TILE = 256


def position():
    space, samp = lax.axis_index("space"), lax.axis_index("samp")
    core, z = lax.rem(space, 2), lax.rem(space // 2, 8)
    y_lo, y_hi = space // 16, lax.rem(samp, 2)
    return samp // 2, y_hi * 4 + y_lo, z, core


def device(at, dx=0, dy=0, dz=0, dc=0):
    x, y, z, core = at
    x, y, z = lax.rem(x + dx, XS), lax.rem(y + dy, YS), lax.rem(z + dz, ZS)
    core = lax.rem(core + dc, CORES)
    return {
        "space": (lax.rem(y, 4) * ZS + z) * 2 + core,
        "samp": x * 2 + y // 4,
    }


NEAR = [(dx, dc) for dx in range(XS) for dc in range(CORES) if (dx, dc) != (0, 0)]


def halves(value):
    high = value.astype(bf16)
    return high, (value - high.astype(f32)).astype(bf16)


def nn(a, b):
    return jnp.dot(a, b, preferred_element_type=f32)


def nt(a, b):
    return lax.dot_general(a, b, (((1,), (1,)), ((), ())), preferred_element_type=f32)


def kernel(
    x_hbm, b_hbm, a_hbm, out_v,
    x_v, a_v, basis, bhi, blo, yhi, ylo, diag, dhi, dlo, thi, tlo,
    part, rs_in, rs_sum, z_in, z_sum, y_in, core, shi, slo,
    load_sem, sy, ry, sx, rx, sxf, rxf, sp, rp, spf, rpf,
    s_rs, r_rs, s_z, r_z, s_y, r_y, s_ag, r_ag,
):
    at = position()
    x, y, z, c = at
    mine = y // 4
    other = 1 - mine

    loads = [
        pltpu.make_async_copy(b_hbm, basis.at[mine, x], load_sem.at[0]),
        pltpu.make_async_copy(a_hbm, a_v, load_sem.at[1]),
        pltpu.make_async_copy(x_hbm, x_v, load_sem.at[2]),
    ]
    for load in loads:
        load.start()

    barrier = pltpu.get_barrier_semaphore()
    partners = [dict(dx=dx, dc=dc) for dx, dc in NEAR]
    partners += [dict(dz=d) for d in range(1, ZS)] + [dict(dy=d) for d in range(1, YS)]
    for partner in partners:
        pl.semaphore_signal(
            barrier, inc=1, device_id=device(at, **partner), device_id_type=MESH
        )
    diag[...] = jnp.zeros_like(diag)
    pl.semaphore_wait(barrier, len(partners))

    started = []

    def remote(src, dst, send, recv, **offset):
        return pltpu.make_async_remote_copy(
            src_ref=src,
            dst_ref=dst,
            send_sem=send,
            recv_sem=recv,
            device_id=device(at, **offset),
            device_id_type=MESH,
        )

    def go(copy):
        copy.start()
        started.append(copy)

    step = (1, XS - 1)

    def own_rows(d, half, block_x):
        ref = basis.at[mine, block_x, pl.ds(half * 16, 16)]
        return remote(ref, ref, sx.at[d, half], rx.at[d, half], dx=step[d])

    def own_forward(d, block_x):
        ref = basis.at[mine, block_x, pl.ds(d * 16, 16)]
        return remote(ref, ref, sxf.at[d], rxf.at[d], dx=step[d])

    def across(h, chunk):
        ref = basis.at[h, x, pl.ds(chunk * 8, 8)]
        return remote(ref, ref, sy.at[chunk], ry.at[chunk], dy=4)

    def partner_rows(d, chunk, block_x):
        ref = basis.at[other, block_x, pl.ds(chunk * 8, 8)]
        return remote(ref, ref, sp.at[d, chunk], rp.at[d, chunk], dx=step[d])

    def partner_forward(d, i, block_x):
        ref = basis.at[other, block_x, pl.ds((d * 2 + i) * 8, 8)]
        return remote(ref, ref, spf.at[d, i], rpf.at[d, i], dx=step[d])

    before = (lax.rem(x + XS - 1, XS), lax.rem(x + 1, XS))
    far = lax.rem(x + 2, XS)

    loads[0].wait()
    for chunk in range(CHUNKS):
        go(across(mine, chunk))
    for d in range(2):
        go(own_rows(d, d, x))
    for d in range(2):
        go(own_rows(d, 1 - d, x))

    loads[1].wait()
    for t in range(4):
        diag[pl.ds(t * 64, 64), pl.ds(t * 64, 64)] = a_v[...]
    spreader = diag[...]
    dhi[...], dlo[...] = halves(spreader)
    thi[...], tlo[...] = halves(spreader.T)
    loads[2].wait()

    def reduce_samples(j, carry):
        m = pl.ds(pl.multiple_of(j * TILE, TILE), TILE)
        high, low = halves(x_v[:, :, m].reshape(256, TILE))
        y_part = nn(thi[...], high) + nn(thi[...], low) + nn(tlo[...], high)
        yhi[:, m], ylo[:, m] = halves(y_part)
        return carry

    lax.fori_loop(0, 2048 // TILE, reduce_samples, 0)

    for d in range(2):
        own_rows(d, d, before[d]).wait_recv()
        go(own_forward(d, before[d]))

    def send_partner(chunk):
        across(other, chunk).wait_recv()
        for d in range(2):
            go(partner_rows(d, chunk, x))

    def contract(h):
        def body(j, total):
            m = pl.ds(pl.multiple_of(j * 512, 512), 512)
            high, low = halves(basis[h, :, :, m].reshape(128, 512))
            bhi[h, :, m] = high
            blo[h, :, m] = low
            return total + nt(high, yhi[:, m]) + nt(high, ylo[:, m]) + nt(low, yhi[:, m])

        total = lax.fori_loop(0, 4, body, jnp.zeros((128, 256), f32))
        part[h] = total.reshape(XS, CORES, 16, 256)

    def scatter(h, i):
        dx, dc = NEAR[i]
        src = part.at[h, lax.rem(x + dx, XS), lax.rem(c + dc, CORES)]
        return remote(src, rs_in.at[h, i], s_rs.at[h, i], r_rs.at[h, i], dx=dx, dc=dc)

    def along_z(h, i):
        return remote(rs_sum.at[h], z_in.at[h, i], s_z.at[h, i], r_z.at[h, i], dz=i + 1)

    def along_y(h, i):
        return remote(z_sum.at[h], y_in.at[h, i], s_y.at[h, i], r_y.at[h, i], dy=i + 1)

    def start_scatter(h):
        for i in range(7):
            go(scatter(h, i))

    def scatter_to_z(h):
        for i in range(7):
            scatter(h, i).wait_recv()
        rs_sum[h] = part[h, x, c] + jnp.sum(rs_in[h], axis=0)
        for i in range(7):
            go(along_z(h, i))

    def z_to_y(h):
        for i in range(7):
            along_z(h, i).wait_recv()
        z_sum[h] = rs_sum[h] + jnp.sum(z_in[h], axis=0)
        for i in range(7):
            go(along_y(h, i))

    send_partner(0)
    send_partner(1)
    for d in range(2):
        own_rows(d, 1 - d, before[d]).wait_recv()
        own_forward(d, far).wait_recv()
    contract(mine)
    start_scatter(mine)
    send_partner(2)
    scatter_to_z(mine)
    send_partner(3)
    for i in range(2):
        for d in range(2):
            partner_rows(d, d * 2 + i, before[d]).wait_recv()
            go(partner_forward(d, i, before[d]))
    z_to_y(mine)
    for i in range(2):
        for d in range(2):
            partner_rows(d, (1 - d) * 2 + i, before[d]).wait_recv()
            partner_forward(d, i, far).wait_recv()
    contract(other)
    start_scatter(other)
    scatter_to_z(other)
    z_to_y(other)

    for h in range(2):
        for i in range(7):
            along_y(h, i).wait_recv()
        core[h, x, c] = z_sum[h] + jnp.sum(y_in[h], axis=0)

    def gather(i):
        dx, dc = NEAR[i]
        ref = core.at[:, x, c]
        return remote(ref, ref, s_ag.at[i], r_ag.at[i], dx=dx, dc=dc)

    for i in range(7):
        go(gather(i))
    for i in range(7):
        gather(i).wait_recv()

    chi, clo = halves(core[...].reshape(256, 256))
    spread = nt(dhi[...], chi) + nt(dhi[...], clo) + nt(dlo[...], chi)
    shi[...], slo[...] = halves(spread)

    for j in range(2048 // TILE):
        m = pl.ds(j * TILE, TILE)
        high, low = bhi[:, :, m].reshape(256, TILE), blo[:, :, m].reshape(256, TILE)
        removed = nn(shi[...], high) + nn(shi[...], low) + nn(slo[...], high)
        out_v[:, :, m] = x_v[:, :, m] - removed.reshape(4, 64, TILE)
    for copy in started:
        copy.wait_send()


def shards(snapshots, space_basis, sample_basis):
    vmem = pltpu.VMEM
    dma = pltpu.SemaphoreType.DMA
    hbm = pl.BlockSpec(memory_space=pltpu.HBM)
    return pl.pallas_call(
        kernel,
        name="deflate",
        out_shape=jax.ShapeDtypeStruct((4, 64, 2048), f32),
        in_specs=[hbm] * 3,
        out_specs=pl.BlockSpec(memory_space=pltpu.VMEM),
        scratch_shapes=[
            vmem((4, 64, 2048), f32),
            vmem((64, 64), f32),
            vmem((2, XS, 32, 2048), f32),
            vmem((2, 128, 2048), bf16),
            vmem((2, 128, 2048), bf16),
            vmem((256, 2048), bf16),
            vmem((256, 2048), bf16),
            vmem((256, 256), f32),
            vmem((256, 256), bf16),
            vmem((256, 256), bf16),
            vmem((256, 256), bf16),
            vmem((256, 256), bf16),
            vmem((2, XS, CORES, 16, 256), f32),
            vmem((2, 7, 16, 256), f32),
            vmem((2, 16, 256), f32),
            vmem((2, 7, 16, 256), f32),
            vmem((2, 16, 256), f32),
            vmem((2, 7, 16, 256), f32),
            vmem((2, XS, CORES, 16, 256), f32),
            vmem((256, 256), bf16),
            vmem((256, 256), bf16),
            dma((3,)),
            dma((CHUNKS,)), dma((CHUNKS,)),
            dma((2, 2)), dma((2, 2)),
            dma((2,)), dma((2,)),
            dma((2, CHUNKS)), dma((2, CHUNKS)),
            dma((2, 2)), dma((2, 2)),
            dma((2, 7)), dma((2, 7)),
            dma((2, 7)), dma((2, 7)),
            dma((2, 7)), dma((2, 7)),
            dma((7,)), dma((7,)),
        ],
        compiler_params=pltpu.CompilerParams(
            collective_id=0, has_side_effects=True, vmem_limit_bytes=32 * 2**20
        ),
    )(*(pltpu.with_memory_space_constraint(a, pltpu.HBM) for a in (snapshots, space_basis, sample_basis)))


def solution(mesh):
    return jax.shard_map(
        shards,
        mesh=mesh,
        in_specs=(P(None, "samp", "space"), P("samp", "space"), P("samp", None)),
        out_specs=P(None, "samp", "space"),
        check_vma=False,
    )
```

```python
import jax
import jax.numpy as jnp
from jax import lax
from jax.experimental import pallas as pl
from jax.experimental.pallas import tpu as pltpu
from jax.sharding import PartitionSpec as P

MESH = pl.DeviceIdType.MESH
f32, bf16 = jnp.float32, jnp.bfloat16
XS, YS, ZS, CORES = 4, 8, 8, 2
CHUNKS = 4
FORWARDED = 4
SPLIT = 3
WINDOW = 3
TILE = 256


def position():
    space, samp = lax.axis_index("space"), lax.axis_index("samp")
    core, z = lax.rem(space, 2), lax.rem(lax.div(space, 2), ZS)
    y_lo, y_hi = lax.div(space, 2 * ZS), lax.rem(samp, 2)
    return lax.div(samp, 2), y_hi * 4 + y_lo, z, core


def device(at, dx=0, dy=0, dz=0, dc=0):
    x, y, z, core = at
    where = {}
    if isinstance(dy, int) and dy == 0:
        space, samp = lax.axis_index("space"), lax.axis_index("samp")
    else:
        y_new = lax.rem(y + dy, YS)
        space = (lax.rem(y_new, 4) * ZS + z) * 2 + core
        samp = x * 2 + lax.div(y_new, 4)
        where = {"space": space, "samp": samp}
    if not (isinstance(dx, int) and dx == 0):
        where["samp"] = samp + (lax.rem(x + dx, XS) - x) * 2
    if not (isinstance(dz, int) and dz == 0):
        space = space + (lax.rem(z + dz, ZS) - z) * 2
        where["space"] = space
    if dc:
        where["space"] = space + 1 - core * 2
    return where


NEAR = [(dx, dc) for dx in range(XS) for dc in range(CORES) if (dx, dc) != (0, 0)]


def halves(value):
    high = value.astype(bf16)
    return high, (value - high.astype(f32)).astype(bf16)


def nn(a, b):
    return jnp.dot(a, b, preferred_element_type=f32)


def nt(a, b):
    return lax.dot_general(a, b, (((1,), (1,)), ((), ())), preferred_element_type=f32)


def kernel(
    x_hbm, b_hbm, a_hbm, out_v,
    x_v, a_v, basis, bhi, blo, yhi, ylo, diag, dhi, dlo, thi, tlo,
    part, rs_in, rs_sum, z_in, z_sum, y_in, core, matrix, shi, slo,
    load_sem, sy, ry, sx, rx, sxf, rxf, sp, rp, s_rs, r_rs, s_z, r_z, s_y, r_y, s_ag, r_ag,
):
    at = position()
    x, y, z, c = at
    mine = lax.div(y, 4)
    other = 1 - mine

    loads = [
        pltpu.make_async_copy(
            b_hbm.at[pl.ds(i * 8, 8)], basis.at[mine, i, x], load_sem.at[i]
        )
        for i in range(CHUNKS)
    ]
    load_a = pltpu.make_async_copy(a_hbm, a_v, load_sem.at[CHUNKS])
    load_x = pltpu.make_async_copy(x_hbm, x_v, load_sem.at[CHUNKS + 1])
    for load in (*loads, load_a, load_x):
        load.start()

    barrier = pltpu.get_barrier_semaphore()
    partners = [dict(dy=d) for d in (4, 1, 7, 2, 6, 3, 5)]
    partners += [dict(dx=dx, dc=dc) for dx, dc in NEAR]
    partners += [dict(dz=d) for d in range(1, ZS)]
    for partner in partners:
        pl.semaphore_signal(
            barrier, inc=1, device_id=device(at, **partner), device_id_type=MESH
        )
    diag[...] = jnp.zeros_like(diag)
    for load in loads:
        load.wait()
    pl.semaphore_wait(barrier, len(partners))

    started = []

    def remote(src, dst, send, recv, **offset):
        return pltpu.make_async_remote_copy(
            src_ref=src,
            dst_ref=dst,
            send_sem=send,
            recv_sem=recv,
            device_id=device(at, **offset),
            device_id_type=MESH,
        )

    def go(copy):
        copy.start()
        started.append(copy)

    def drain(keep=0):
        while len(started) > keep:
            started.pop(0).wait_send()

    def across(h, i):
        ref = basis.at[h, i, x]
        return remote(ref, ref, sy.at[i], ry.at[i], dy=4)

    step = (1, XS - 1)
    before = (lax.rem(x + XS - 1, XS), lax.rem(x + 1, XS))
    far = lax.rem(x + 2, XS)

    def own_rows(d, half, block_x):
        ref = basis.at[mine, pl.ds(half * 2, 2), block_x]
        return remote(ref, ref, sx.at[d, half], rx.at[d, half], dx=step[d])

    def own_forward(d, block_x):
        ref = basis.at[mine, pl.ds(d * 2, 2), block_x]
        return remote(ref, ref, sxf.at[d], rxf.at[d], dx=step[d])

    def partner_rows(d, i, block_x):
        ref = basis.at[other, i, block_x]
        return remote(ref, ref, sp.at[i, d], rp.at[i, d], dx=step[d])

    def partner_far(i, block_x):
        ref = basis.at[other, i, block_x]
        dx = step[i % 2] if i < FORWARDED else 2
        return remote(ref, ref, sp.at[i, 2], rp.at[i, 2], dx=dx)

    for i in range(WINDOW):
        go(across(mine, i))
    for d in range(2):
        go(own_rows(d, d, x))
    for d in range(2):
        go(own_rows(d, 1 - d, x))

    load_a.wait()
    for t in range(4):
        diag[pl.ds(t * 64, 64), pl.ds(t * 64, 64)] = a_v[...]
    spreader = diag[...]
    dhi[...], dlo[...] = halves(spreader)
    thi[...], tlo[...] = halves(spreader.T)
    load_x.wait()

    def reduce_samples(j, carry):
        m = pl.ds(pl.multiple_of(j * TILE, TILE), TILE)
        high, low = halves(x_v[:, :, m].reshape(256, TILE))
        y_part = nn(thi[...], high) + nn(thi[...], low) + nn(tlo[...], high)
        yhi[:, m], ylo[:, m] = halves(y_part)
        return carry

    lax.fori_loop(0, 2048 // TILE, reduce_samples, 0)

    def send_partner(i):
        across(other, i).wait_recv()
        for d in range(2):
            go(partner_rows(d, i, x))
        if i >= FORWARDED:
            go(partner_far(i, x))
        if i + WINDOW < CHUNKS:
            go(across(mine, i + WINDOW))

    def contract(h, first, count):
        rows = count * 32

        def body(j, total):
            m = pl.ds(pl.multiple_of(j * 512, 512), 512)
            chunks = pl.ds(first, count)
            high, low = halves(basis[h, chunks, :, :, m].reshape(rows, 512))
            bhi[h, pl.ds(first * 32, rows), m] = high
            blo[h, pl.ds(first * 32, rows), m] = low
            return total + nt(high, yhi[:, m]) + nt(high, ylo[:, m]) + nt(low, yhi[:, m])

        total = lax.fori_loop(0, 4, body, jnp.zeros((rows, 256), f32))
        for half in range(CORES):
            part[h, half, pl.ds(first, count)] = total[
                :, half * 128 : half * 128 + 128
            ].reshape(count, XS, 8, 128)

    def scatter(batch, i):
        h, first, count, b = batch
        dx, dc = NEAR[i]
        chunks = pl.ds(first, count)
        src = part.at[h, lax.rem(c + dc, CORES), chunks, lax.rem(x + dx, XS)]
        sems = s_rs.at[h, b, i], r_rs.at[h, b, i]
        return remote(src, rs_in.at[h, i, chunks], *sems, dx=dx, dc=dc)

    def along_z(batch, i):
        h, first, count, b = batch
        chunks = pl.ds(first, count)
        sems = s_z.at[h, b, i], r_z.at[h, b, i]
        return remote(rs_sum.at[h, chunks], z_in.at[h, i, chunks], *sems, dz=i + 1)

    def along_y(batch, i):
        h, first, count, b = batch
        chunks = pl.ds(first, count)
        sems = s_y.at[h, b, i], r_y.at[h, b, i]
        return remote(z_sum.at[h, chunks], y_in.at[h, i, chunks], *sems, dy=i + 1)

    def start_scatter(batch):
        for i in range(7):
            go(scatter(batch, i))

    def scatter_to_z(batch):
        h, first, count, _ = batch
        chunks = pl.ds(first, count)
        for i in range(7):
            scatter(batch, i).wait_recv()
        rs_sum[h, chunks] = part[h, c, chunks, x] + jnp.sum(rs_in[h, :, chunks], axis=0)
        for i in range(7):
            go(along_z(batch, i))

    def z_to_y(batch):
        h, first, count, _ = batch
        chunks = pl.ds(first, count)
        for i in range(7):
            along_z(batch, i).wait_recv()
        z_sum[h, chunks] = rs_sum[h, chunks] + jnp.sum(z_in[h, :, chunks], axis=0)
        for i in range(7):
            go(along_y(batch, i))

    def pass_on(i):
        if i < FORWARDED:
            partner_rows(i % 2, i, before[i % 2]).wait_recv()
            go(partner_far(i, before[i % 2]))

    def arrived(i):
        for d in range(2):
            if i >= FORWARDED or d != i % 2:
                partner_rows(d, i, before[d]).wait_recv()
        partner_far(i, far).wait_recv()

    early = (mine, 0, CHUNKS, 0)
    late = [(other, 0, SPLIT, 0), (other, SPLIT, CHUNKS - SPLIT, 1)]

    for d in range(2):
        own_rows(d, d, before[d]).wait_recv()
        go(own_forward(d, before[d]))
    send_partner(0)
    for d in range(2):
        own_rows(d, 1 - d, before[d]).wait_recv()
        own_forward(d, far).wait_recv()
    contract(*early[:3])
    start_scatter(early)
    send_partner(1)
    pass_on(0)
    send_partner(2)
    pass_on(1)
    scatter_to_z(early)
    send_partner(3)
    pass_on(2)
    pass_on(3)
    z_to_y(early)
    arrived(0)
    arrived(1)
    arrived(2)
    contract(*late[0][:3])
    start_scatter(late[0])
    arrived(3)
    contract(*late[1][:3])
    start_scatter(late[1])
    scatter_to_z(late[0])
    scatter_to_z(late[1])
    drain(keep=28)
    z_to_y(late[0])
    z_to_y(late[1])
    drain(keep=14)

    for h in range(2):
        for i in range(7):
            source = lax.div(lax.rem(y + YS - 1 - i, YS), 4)
            pl.when(source == h)(along_y((h, 0, CHUNKS, 0), i).wait_recv)

            @pl.when(source != h)
            def _():
                along_y((h, 0, SPLIT, 0), i).wait_recv()
                along_y((h, SPLIT, CHUNKS - SPLIT, 1), i).wait_recv()

        core[x, c, h] = z_sum[h] + jnp.sum(y_in[h], axis=0)

    def gather(i):
        dx, dc = NEAR[i]
        ref = core.at[x, c]
        return remote(ref, ref, s_ag.at[i], r_ag.at[i], dx=dx, dc=dc)

    for i in range(7):
        go(gather(i))
    drain(keep=7)
    for i in range(7):
        gather(i).wait_recv()

    for h in range(2):
        for i in range(CHUNKS):
            for block in range(XS):
                for half in range(CORES):
                    rows = pl.ds(((h * CHUNKS + i) * XS + block) * 8, 8)
                    matrix[rows, pl.ds(half * 128, 128)] = core[block, half, h, i]
    chi, clo = halves(matrix[...])
    spread = nt(dhi[...], chi) + nt(dhi[...], clo) + nt(dlo[...], chi)
    shi[...], slo[...] = halves(spread)

    for j in range(2048 // TILE):
        m = pl.ds(j * TILE, TILE)
        high, low = bhi[:, :, m].reshape(256, TILE), blo[:, :, m].reshape(256, TILE)
        removed = nn(shi[...], high) + nn(shi[...], low) + nn(slo[...], high)
        out_v[:, :, m] = x_v[:, :, m] - removed.reshape(4, 64, TILE)
    drain()


def shards(snapshots, space_basis, sample_basis):
    vmem = pltpu.VMEM
    dma = pltpu.SemaphoreType.DMA
    hbm = pl.BlockSpec(memory_space=pltpu.HBM)
    return pl.pallas_call(
        kernel,
        name="deflate",
        out_shape=jax.ShapeDtypeStruct((4, 64, 2048), f32),
        in_specs=[hbm] * 3,
        out_specs=pl.BlockSpec(memory_space=pltpu.VMEM),
        scratch_shapes=[
            vmem((4, 64, 2048), f32),
            vmem((64, 64), f32),
            vmem((2, CHUNKS, XS, 8, 2048), f32),
            vmem((2, 128, 2048), bf16),
            vmem((2, 128, 2048), bf16),
            vmem((256, 2048), bf16),
            vmem((256, 2048), bf16),
            vmem((256, 256), f32),
            vmem((256, 256), bf16),
            vmem((256, 256), bf16),
            vmem((256, 256), bf16),
            vmem((256, 256), bf16),
            vmem((2, CORES, CHUNKS, XS, 8, 128), f32),
            vmem((2, 7, CHUNKS, 8, 128), f32),
            vmem((2, CHUNKS, 8, 128), f32),
            vmem((2, 7, CHUNKS, 8, 128), f32),
            vmem((2, CHUNKS, 8, 128), f32),
            vmem((2, 7, CHUNKS, 8, 128), f32),
            vmem((XS, CORES, 2, CHUNKS, 8, 128), f32),
            vmem((256, 256), f32),
            vmem((256, 256), bf16),
            vmem((256, 256), bf16),
            dma((CHUNKS + 2,)),
            dma((CHUNKS,)), dma((CHUNKS,)),
            dma((2, 2)), dma((2, 2)),
            dma((2,)), dma((2,)),
            dma((CHUNKS, 3)), dma((CHUNKS, 3)),
            dma((2, 2, 7)), dma((2, 2, 7)),
            dma((2, 2, 7)), dma((2, 2, 7)),
            dma((2, 2, 7)), dma((2, 2, 7)),
            dma((7,)), dma((7,)),
        ],
        compiler_params=pltpu.CompilerParams(
            collective_id=0, has_side_effects=True, vmem_limit_bytes=32 * 2**20
        ),
    )(*(pltpu.with_memory_space_constraint(a, pltpu.HBM) for a in (snapshots, space_basis, sample_basis)))


def solution(mesh):
    return jax.shard_map(
        shards,
        mesh=mesh,
        in_specs=(P(None, "samp", "space"), P("samp", "space"), P("samp", None)),
        out_specs=P(None, "samp", "space"),
        check_vma=False,
    )
```

```python
import jax
import jax.numpy as jnp
from jax import lax
from jax.experimental import pallas as pl
from jax.experimental.pallas import tpu as pltpu
from jax.sharding import PartitionSpec as P

MESH = pl.DeviceIdType.MESH
f32, bf16 = jnp.float32, jnp.bfloat16
XS, YS, ZS, CORES = 4, 8, 8, 2
CHUNKS = 4
FORWARDED = 2
SPLIT = 2
WINDOW = 3
TILE = 256


def position():
    space, samp = lax.axis_index("space"), lax.axis_index("samp")
    core, z = lax.rem(space, 2), lax.rem(lax.div(space, 2), ZS)
    y_lo, y_hi = lax.div(space, 2 * ZS), lax.rem(samp, 2)
    return lax.div(samp, 2), y_hi * 4 + y_lo, z, core


def device(at, dx=0, dy=0, dz=0, dc=0):
    x, y, z, core = at
    where = {}
    if isinstance(dy, int) and dy == 0:
        space, samp = lax.axis_index("space"), lax.axis_index("samp")
    else:
        y_new = lax.rem(y + dy, YS)
        space = (lax.rem(y_new, 4) * ZS + z) * 2 + core
        samp = x * 2 + lax.div(y_new, 4)
        where = {"space": space, "samp": samp}
    if not (isinstance(dx, int) and dx == 0):
        where["samp"] = samp + (lax.rem(x + dx, XS) - x) * 2
    if not (isinstance(dz, int) and dz == 0):
        space = space + (lax.rem(z + dz, ZS) - z) * 2
        where["space"] = space
    if dc:
        where["space"] = space + 1 - core * 2
    return where


NEAR = [(dx, dc) for dx in range(XS) for dc in range(CORES) if (dx, dc) != (0, 0)]

NEAR_ORDER = (4, 3, 2, 6, 1, 5, 0)
FAR_FIRST = (3, 2, 4, 1, 5, 0, 6)


def halves(value):
    high = value.astype(bf16)
    return high, (value - high.astype(f32)).astype(bf16)


def nn(a, b):
    return jnp.dot(a, b, preferred_element_type=f32)


def nt(a, b):
    return lax.dot_general(a, b, (((1,), (1,)), ((), ())), preferred_element_type=f32)


def kernel(
    x_hbm, b_hbm, a_hbm, out_v,
    x_v, a_v, basis, bhi, blo, yhi, ylo, diag, dhi, dlo, thi, tlo,
    part, rs_in, rs_sum, z_in, z_sum, y_in, core, matrix, spread,
    load_sem, sy, ry, sx, rx, sxf, rxf, sp, rp, s_rs, r_rs, s_z, r_z, s_y, r_y, s_ag, r_ag,
):
    at = position()
    x, y, z, c = at
    mine = lax.div(y, 4)
    other = 1 - mine

    loads = [
        pltpu.make_async_copy(
            b_hbm.at[pl.ds(i * 8, 8)], basis.at[mine, i, x], load_sem.at[i]
        )
        for i in range(CHUNKS)
    ]
    load_a = pltpu.make_async_copy(a_hbm, a_v, load_sem.at[CHUNKS])
    load_x = pltpu.make_async_copy(x_hbm, x_v, load_sem.at[CHUNKS + 1])
    for load in (*loads, load_a, load_x):
        load.start()

    barrier = pltpu.get_barrier_semaphore()
    partners = [dict(dy=d) for d in (4, 1, 7, 2, 6, 3, 5)]
    partners += [dict(dx=dx, dc=dc) for dx, dc in NEAR]
    partners += [dict(dz=d) for d in range(1, ZS)]
    for partner in partners:
        pl.semaphore_signal(
            barrier, inc=1, device_id=device(at, **partner), device_id_type=MESH
        )
    diag[...] = jnp.zeros_like(diag)
    for load in loads:
        load.wait()
    pl.semaphore_wait(barrier, len(partners))

    started = []

    def remote(src, dst, send, recv, **offset):
        return pltpu.make_async_remote_copy(
            src_ref=src,
            dst_ref=dst,
            send_sem=send,
            recv_sem=recv,
            device_id=device(at, **offset),
            device_id_type=MESH,
        )

    def go(copy):
        copy.start()
        started.append(copy)

    def drain(keep=0):
        while len(started) > keep:
            started.pop(0).wait_send()

    def across(h, i):
        ref = basis.at[h, i, x]
        return remote(ref, ref, sy.at[i], ry.at[i], dy=4)

    step = (1, XS - 1)
    before = (lax.rem(x + XS - 1, XS), lax.rem(x + 1, XS))
    far = lax.rem(x + 2, XS)

    def own_rows(d, half, block_x):
        ref = basis.at[mine, pl.ds(half * 2, 2), block_x]
        return remote(ref, ref, sx.at[d, half], rx.at[d, half], dx=step[d])

    def own_forward(d, block_x):
        ref = basis.at[mine, pl.ds(d * 2, 2), block_x]
        return remote(ref, ref, sxf.at[d], rxf.at[d], dx=step[d])

    def partner_rows(d, i, block_x):
        ref = basis.at[other, i, block_x]
        return remote(ref, ref, sp.at[i, d], rp.at[i, d], dx=step[d])

    def partner_far(i, block_x):
        ref = basis.at[other, i, block_x]
        dx = step[i % 2] if i < FORWARDED else 2
        return remote(ref, ref, sp.at[i, 2], rp.at[i, 2], dx=dx)

    for i in range(WINDOW):
        go(across(mine, i))
    for d in range(2):
        go(own_rows(d, d, x))
    for d in range(2):
        go(own_rows(d, 1 - d, x))

    load_a.wait()
    for t in range(4):
        diag[pl.ds(t * 64, 64), pl.ds(t * 64, 64)] = a_v[...]
    spreader = diag[...]
    dhi[...], dlo[...] = halves(spreader)
    thi[...], tlo[...] = halves(spreader.T)
    load_x.wait()

    def reduce_samples(j, carry):
        m = pl.ds(pl.multiple_of(j * TILE, TILE), TILE)
        high, low = halves(x_v[:, :, m].reshape(256, TILE))
        y_part = nn(thi[...], high) + nn(thi[...], low) + nn(tlo[...], high)
        yhi[:, m], ylo[:, m] = halves(y_part)
        return carry

    lax.fori_loop(0, 2048 // TILE, reduce_samples, 0)

    def send_partner(i):
        across(other, i).wait_recv()
        for d in range(2):
            go(partner_rows(d, i, x))
        if i >= FORWARDED:
            go(partner_far(i, x))
        if i + WINDOW < CHUNKS:
            go(across(mine, i + WINDOW))

    def contract(h, first, count):
        rows = count * 32

        def body(j, total):
            m = pl.ds(pl.multiple_of(j * 512, 512), 512)
            chunks = pl.ds(first, count)
            high, low = halves(basis[h, chunks, :, :, m].reshape(rows, 512))
            parts = pl.ds(first // SPLIT, count // SPLIT)
            bhi[parts, h, :, m] = high.reshape(count // SPLIT, SPLIT * 32, 512)
            blo[parts, h, :, m] = low.reshape(count // SPLIT, SPLIT * 32, 512)
            return total + nt(high, yhi[:, m]) + nt(high, ylo[:, m]) + nt(low, yhi[:, m])

        total = lax.fori_loop(0, 4, body, jnp.zeros((rows, 256), f32))
        for half in range(CORES):
            part[h, half, pl.ds(first, count)] = total[
                :, half * 128 : half * 128 + 128
            ].reshape(count, XS, 8, 128)

    def scatter(batch, i):
        h, first, count, b = batch
        dx, dc = NEAR[i]
        chunks = pl.ds(first, count)
        src = part.at[h, lax.rem(c + dc, CORES), chunks, lax.rem(x + dx, XS)]
        sems = s_rs.at[h, b, i], r_rs.at[h, b, i]
        return remote(src, rs_in.at[h, i, chunks], *sems, dx=dx, dc=dc)

    def along_z(batch, i):
        h, first, count, b = batch
        chunks = pl.ds(first, count)
        sems = s_z.at[h, b, i], r_z.at[h, b, i]
        return remote(rs_sum.at[h, chunks], z_in.at[h, i, chunks], *sems, dz=i + 1)

    def along_y(batch, i):
        h, first, count, b = batch
        chunks = pl.ds(first, count)
        sems = s_y.at[h, b, i], r_y.at[h, b, i]
        return remote(z_sum.at[h, chunks], y_in.at[h, i, chunks], *sems, dy=i + 1)

    def start_scatter(batch):
        for i in NEAR_ORDER:
            go(scatter(batch, i))

    def scatter_to_z(batch):
        h, first, count, _ = batch
        chunks = pl.ds(first, count)
        for i in range(7):
            scatter(batch, i).wait_recv()
        rs_sum[h, chunks] = part[h, c, chunks, x] + jnp.sum(rs_in[h, :, chunks], axis=0)
        for i in FAR_FIRST:
            go(along_z(batch, i))

    def z_to_y(batch):
        h, first, count, _ = batch
        chunks = pl.ds(first, count)
        for i in range(7):
            along_z(batch, i).wait_recv()
        z_sum[h, chunks] = rs_sum[h, chunks] + jnp.sum(z_in[h, :, chunks], axis=0)
        for i in FAR_FIRST:
            go(along_y(batch, i))

    def pass_on(i):
        if i < FORWARDED:
            partner_rows(i % 2, i, before[i % 2]).wait_recv()
            go(partner_far(i, before[i % 2]))

    def arrived(i):
        for d in range(2):
            if i >= FORWARDED or d != i % 2:
                partner_rows(d, i, before[d]).wait_recv()
        partner_far(i, far).wait_recv()

    early = (mine, 0, CHUNKS, 0)
    late = [(other, 0, SPLIT, 0), (other, SPLIT, CHUNKS - SPLIT, 1)]

    for d in range(2):
        own_rows(d, d, before[d]).wait_recv()
        go(own_forward(d, before[d]))
    send_partner(0)
    for d in range(2):
        own_rows(d, 1 - d, before[d]).wait_recv()
        own_forward(d, far).wait_recv()
    contract(*early[:3])
    start_scatter(early)
    send_partner(1)
    pass_on(0)
    send_partner(2)
    pass_on(1)
    scatter_to_z(early)
    send_partner(3)
    pass_on(2)
    pass_on(3)
    z_to_y(early)
    arrived(0)
    arrived(1)
    contract(*late[0][:3])
    start_scatter(late[0])
    arrived(2)
    arrived(3)
    contract(*late[1][:3])
    start_scatter(late[1])
    scatter_to_z(late[0])
    scatter_to_z(late[1])
    drain(keep=28)
    z_to_y(late[0])
    z_to_y(late[1])
    drain(keep=14)

    def sum_over_y(b):
        chunks = pl.ds(b * SPLIT, SPLIT)
        for h in range(2):
            for i in range(7):
                source = lax.div(lax.rem(y + YS - 1 - i, YS), 4)
                if b == 0:
                    pl.when(source == h)(along_y((h, 0, CHUNKS, 0), i).wait_recv)
                pl.when(source != h)(along_y((h, b * SPLIT, SPLIT, b), i).wait_recv)
            core[x, c, h, chunks] = z_sum[h, chunks] + jnp.sum(y_in[h, :, chunks], axis=0)

    def gather(b, i):
        dx, dc = NEAR[i]
        ref = core.at[x, c, :, pl.ds(b * SPLIT, SPLIT)]
        return remote(ref, ref, s_ag.at[b, i], r_ag.at[b, i], dx=dx, dc=dc)

    for b in range(2):
        sum_over_y(b)
        for i in NEAR_ORDER:
            go(gather(b, i))
    drain(keep=14)

    for b in range(2):
        for i in range(7):
            gather(b, i).wait_recv()
        for h in range(2):
            for i in range(SPLIT):
                for block in range(XS):
                    for half in range(CORES):
                        rows = pl.ds(((h * SPLIT + i) * XS + block) * 8, 8)
                        matrix[rows, pl.ds(half * 128, 128)] = core[
                            block, half, h, b * SPLIT + i
                        ]
        chi, clo = halves(matrix[...])
        high, low = halves(nt(dhi[...], chi) + nt(dhi[...], clo) + nt(dlo[...], chi))
        spread[...] = jnp.concatenate([high, low, high], axis=1)
        for j in range(2048 // TILE):
            m = pl.ds(j * TILE, TILE)
            high, low = bhi[b, :, :, m].reshape(128, TILE), blo[b, :, :, m].reshape(128, TILE)
            removed = nn(spread[...], jnp.concatenate([high, high, low], axis=0))
            kept = x_v if b == 0 else out_v
            out_v[:, :, m] = kept[:, :, m] - removed.reshape(4, 64, TILE)
    drain()


def shards(snapshots, space_basis, sample_basis):
    vmem = pltpu.VMEM
    dma = pltpu.SemaphoreType.DMA
    hbm = pl.BlockSpec(memory_space=pltpu.HBM)
    return pl.pallas_call(
        kernel,
        name="deflate",
        out_shape=jax.ShapeDtypeStruct((4, 64, 2048), f32),
        in_specs=[hbm] * 3,
        out_specs=pl.BlockSpec(memory_space=pltpu.VMEM),
        scratch_shapes=[
            vmem((4, 64, 2048), f32),
            vmem((64, 64), f32),
            vmem((2, CHUNKS, XS, 8, 2048), f32),
            vmem((2, 2, SPLIT * 32, 2048), bf16),
            vmem((2, 2, SPLIT * 32, 2048), bf16),
            vmem((256, 2048), bf16),
            vmem((256, 2048), bf16),
            vmem((256, 256), f32),
            vmem((256, 256), bf16),
            vmem((256, 256), bf16),
            vmem((256, 256), bf16),
            vmem((256, 256), bf16),
            vmem((2, CORES, CHUNKS, XS, 8, 128), f32),
            vmem((2, 7, CHUNKS, 8, 128), f32),
            vmem((2, CHUNKS, 8, 128), f32),
            vmem((2, 7, CHUNKS, 8, 128), f32),
            vmem((2, CHUNKS, 8, 128), f32),
            vmem((2, 7, CHUNKS, 8, 128), f32),
            vmem((XS, CORES, 2, CHUNKS, 8, 128), f32),
            vmem((128, 256), f32),
            vmem((256, 384), bf16),
            dma((CHUNKS + 2,)),
            dma((CHUNKS,)), dma((CHUNKS,)),
            dma((2, 2)), dma((2, 2)),
            dma((2,)), dma((2,)),
            dma((CHUNKS, 3)), dma((CHUNKS, 3)),
            dma((2, 2, 7)), dma((2, 2, 7)),
            dma((2, 2, 7)), dma((2, 2, 7)),
            dma((2, 2, 7)), dma((2, 2, 7)),
            dma((2, 7)), dma((2, 7)),
        ],
        compiler_params=pltpu.CompilerParams(
            collective_id=0, has_side_effects=True, vmem_limit_bytes=32 * 2**20
        ),
    )(*(pltpu.with_memory_space_constraint(a, pltpu.HBM) for a in (snapshots, space_basis, sample_basis)))


def solution(mesh):
    return jax.shard_map(
        shards,
        mesh=mesh,
        in_specs=(P(None, "samp", "space"), P("samp", "space"), P("samp", None)),
        out_specs=P(None, "samp", "space"),
        check_vma=False,
    )
```

```python
import jax
import jax.numpy as jnp
from jax import lax
from jax.experimental import pallas as pl
from jax.experimental.pallas import tpu as pltpu
from jax.sharding import PartitionSpec as P

MESH = pl.DeviceIdType.MESH
f32, bf16 = jnp.float32, jnp.bfloat16
XS, YS, ZS, CORES = 4, 8, 8, 2
CHUNKS = 4
FORWARDED = 2
SPLIT = 2
WINDOW = 3
TILE = 256


def position():
    space, samp = lax.axis_index("space"), lax.axis_index("samp")
    core, z = lax.rem(space, 2), lax.rem(lax.div(space, 2), ZS)
    y_lo, y_hi = lax.div(space, 2 * ZS), lax.rem(samp, 2)
    return lax.div(samp, 2), y_hi * 4 + y_lo, z, core


def device(at, dx=0, dy=0, dz=0, dc=0):
    x, y, z, core = at
    where = {}
    if isinstance(dy, int) and dy == 0:
        space, samp = lax.axis_index("space"), lax.axis_index("samp")
    else:
        y_new = lax.rem(y + dy, YS)
        space = (lax.rem(y_new, 4) * ZS + z) * 2 + core
        samp = x * 2 + lax.div(y_new, 4)
        where = {"space": space, "samp": samp}
    if not (isinstance(dx, int) and dx == 0):
        where["samp"] = samp + (lax.rem(x + dx, XS) - x) * 2
    if not (isinstance(dz, int) and dz == 0):
        space = space + (lax.rem(z + dz, ZS) - z) * 2
        where["space"] = space
    if dc:
        where["space"] = space + 1 - core * 2
    return where


NEAR = [(dx, dc) for dx in range(XS) for dc in range(CORES) if (dx, dc) != (0, 0)]

NEAR_ORDER = (4, 3, 2, 6, 1, 5, 0)
FAR_FIRST = (3, 2, 4, 1, 5, 0, 6)


def halves(value):
    high = value.astype(bf16)
    return high, (value - high.astype(f32)).astype(bf16)


def nn(a, b):
    return jnp.dot(a, b, preferred_element_type=f32)


def nt(a, b):
    return lax.dot_general(a, b, (((1,), (1,)), ((), ())), preferred_element_type=f32)


def kernel(
    x_hbm, b_hbm, a_hbm, out_v,
    x_v, a_v, basis, bhi, blo, yhi, ylo, diag, dhi, dlo, thi, tlo,
    part, rs_in, rs_sum, z_in, z_sum, y_in, core, matrix, spread,
    load_sem, sy, ry, sx, rx, sxf, rxf, sp, rp, s_rs, r_rs, s_z, r_z, s_y, r_y, s_ag, r_ag,
):
    at = position()
    x, y, z, c = at
    mine = lax.div(y, 4)
    other = 1 - mine

    loads = [
        pltpu.make_async_copy(
            b_hbm.at[pl.ds(i * 8, 8)], basis.at[mine, i, x], load_sem.at[i]
        )
        for i in range(CHUNKS)
    ]
    load_a = pltpu.make_async_copy(a_hbm, a_v, load_sem.at[CHUNKS])
    load_x = pltpu.make_async_copy(x_hbm, x_v, load_sem.at[CHUNKS + 1])
    for load in (*loads, load_a, load_x):
        load.start()

    barrier = pltpu.get_barrier_semaphore()
    partners = [dict(dy=d) for d in (4, 1, 7, 2, 6, 3, 5)]
    partners += [dict(dx=dx, dc=dc) for dx, dc in NEAR]
    partners += [dict(dz=d) for d in range(1, ZS)]
    for partner in partners:
        pl.semaphore_signal(
            barrier, inc=1, device_id=device(at, **partner), device_id_type=MESH
        )
    diag[...] = jnp.zeros_like(diag)
    for load in loads:
        load.wait()
    pl.semaphore_wait(barrier, len(partners))

    started = []

    def remote(src, dst, send, recv, **offset):
        return pltpu.make_async_remote_copy(
            src_ref=src,
            dst_ref=dst,
            send_sem=send,
            recv_sem=recv,
            device_id=device(at, **offset),
            device_id_type=MESH,
        )

    def go(copy):
        copy.start()
        started.append(copy)

    def drain(keep=0):
        while len(started) > keep:
            started.pop(0).wait_send()

    def across(h, i):
        ref = basis.at[h, i, x]
        return remote(ref, ref, sy.at[i], ry.at[i], dy=4)

    step = (1, XS - 1)
    before = (lax.rem(x + XS - 1, XS), lax.rem(x + 1, XS))
    far = lax.rem(x + 2, XS)

    def own_rows(d, half, block_x):
        ref = basis.at[mine, pl.ds(half * 2, 2), block_x]
        return remote(ref, ref, sx.at[d, half], rx.at[d, half], dx=step[d])

    def own_far(half, block_x):
        ref = basis.at[mine, pl.ds(half * 2, 2), block_x]
        return remote(ref, ref, sxf.at[half], rxf.at[half], dx=2)

    def partner_rows(d, i, block_x):
        ref = basis.at[other, i, block_x]
        return remote(ref, ref, sp.at[i, d], rp.at[i, d], dx=step[d])

    def partner_far(i, block_x):
        ref = basis.at[other, i, block_x]
        dx = step[i % 2] if i < FORWARDED else 2
        return remote(ref, ref, sp.at[i, 2], rp.at[i, 2], dx=dx)

    for i in range(WINDOW):
        go(across(mine, i))
    for d in range(2):
        go(own_rows(d, d, x))
    for half in range(2):
        go(own_far(half, x))
    for d in range(2):
        go(own_rows(d, 1 - d, x))

    load_a.wait()
    for t in range(4):
        diag[pl.ds(t * 64, 64), pl.ds(t * 64, 64)] = a_v[...]
    spreader = diag[...]
    dhi[...], dlo[...] = halves(spreader)
    thi[...], tlo[...] = halves(spreader.T)
    load_x.wait()

    def reduce_samples(j, carry):
        m = pl.ds(pl.multiple_of(j * TILE, TILE), TILE)
        high, low = halves(x_v[:, :, m].reshape(256, TILE))
        y_part = nn(thi[...], high) + nn(thi[...], low) + nn(tlo[...], high)
        yhi[:, m], ylo[:, m] = halves(y_part)
        return carry

    lax.fori_loop(0, 2048 // TILE, reduce_samples, 0)

    def send_partner(i):
        across(other, i).wait_recv()
        for d in range(2):
            go(partner_rows(d, i, x))
        if i >= FORWARDED:
            go(partner_far(i, x))
        if i + WINDOW < CHUNKS:
            go(across(mine, i + WINDOW))

    def contract(h, first, count):
        rows = count * 32

        def body(j, total):
            m = pl.ds(pl.multiple_of(j * 512, 512), 512)
            chunks = pl.ds(first, count)
            high, low = halves(basis[h, chunks, :, :, m].reshape(rows, 512))
            parts = pl.ds(first // SPLIT, count // SPLIT)
            bhi[parts, h, :, m] = high.reshape(count // SPLIT, SPLIT * 32, 512)
            blo[parts, h, :, m] = low.reshape(count // SPLIT, SPLIT * 32, 512)
            return total + nt(high, yhi[:, m]) + nt(high, ylo[:, m]) + nt(low, yhi[:, m])

        total = lax.fori_loop(0, 4, body, jnp.zeros((rows, 256), f32))
        for half in range(CORES):
            part[h, half, pl.ds(first, count)] = total[
                :, half * 128 : half * 128 + 128
            ].reshape(count, XS, 8, 128)

    def scatter(batch, i):
        h, first, count, b = batch
        dx, dc = NEAR[i]
        chunks = pl.ds(first, count)
        src = part.at[h, lax.rem(c + dc, CORES), chunks, lax.rem(x + dx, XS)]
        sems = s_rs.at[h, b, i], r_rs.at[h, b, i]
        return remote(src, rs_in.at[h, i, chunks], *sems, dx=dx, dc=dc)

    def along_z(batch, i):
        h, first, count, b = batch
        chunks = pl.ds(first, count)
        sems = s_z.at[h, b, i], r_z.at[h, b, i]
        return remote(rs_sum.at[h, chunks], z_in.at[h, i, chunks], *sems, dz=i + 1)

    def along_y(batch, i):
        h, first, count, b = batch
        chunks = pl.ds(first, count)
        sems = s_y.at[h, b, i], r_y.at[h, b, i]
        return remote(z_sum.at[h, chunks], y_in.at[h, i, chunks], *sems, dy=i + 1)

    def start_scatter(batch):
        for i in NEAR_ORDER:
            go(scatter(batch, i))

    def scatter_to_z(batch):
        h, first, count, _ = batch
        chunks = pl.ds(first, count)
        for i in range(7):
            scatter(batch, i).wait_recv()
        rs_sum[h, chunks] = part[h, c, chunks, x] + jnp.sum(rs_in[h, :, chunks], axis=0)
        for i in FAR_FIRST:
            go(along_z(batch, i))

    def z_to_y(batch):
        h, first, count, _ = batch
        chunks = pl.ds(first, count)
        for i in range(7):
            along_z(batch, i).wait_recv()
        z_sum[h, chunks] = rs_sum[h, chunks] + jnp.sum(z_in[h, :, chunks], axis=0)
        for i in FAR_FIRST:
            go(along_y(batch, i))

    def pass_on(i):
        if i < FORWARDED:
            partner_rows(i % 2, i, before[i % 2]).wait_recv()
            go(partner_far(i, before[i % 2]))

    def arrived(i):
        for d in range(2):
            if i >= FORWARDED or d != i % 2:
                partner_rows(d, i, before[d]).wait_recv()
        partner_far(i, far).wait_recv()

    early = (mine, 0, CHUNKS, 0)
    late = [(other, 0, SPLIT, 0), (other, SPLIT, CHUNKS - SPLIT, 1)]

    send_partner(0)
    for d in range(2):
        own_rows(d, d, before[d]).wait_recv()
        own_rows(d, 1 - d, before[d]).wait_recv()
        own_far(d, far).wait_recv()
    contract(*early[:3])
    start_scatter(early)
    send_partner(1)
    pass_on(0)
    send_partner(2)
    pass_on(1)
    scatter_to_z(early)
    send_partner(3)
    pass_on(2)
    pass_on(3)
    z_to_y(early)
    arrived(0)
    arrived(1)
    contract(*late[0][:3])
    start_scatter(late[0])
    arrived(2)
    arrived(3)
    contract(*late[1][:3])
    start_scatter(late[1])
    scatter_to_z(late[0])
    scatter_to_z(late[1])
    drain(keep=28)
    z_to_y(late[0])
    z_to_y(late[1])
    drain(keep=14)

    def sum_over_y(b):
        chunks = pl.ds(b * SPLIT, SPLIT)
        for h in range(2):
            for i in range(7):
                source = lax.div(lax.rem(y + YS - 1 - i, YS), 4)
                if b == 0:
                    pl.when(source == h)(along_y((h, 0, CHUNKS, 0), i).wait_recv)
                pl.when(source != h)(along_y((h, b * SPLIT, SPLIT, b), i).wait_recv)
            core[x, c, h, chunks] = z_sum[h, chunks] + jnp.sum(y_in[h, :, chunks], axis=0)

    def gather(b, i):
        dx, dc = NEAR[i]
        ref = core.at[x, c, :, pl.ds(b * SPLIT, SPLIT)]
        return remote(ref, ref, s_ag.at[b, i], r_ag.at[b, i], dx=dx, dc=dc)

    for b in range(2):
        sum_over_y(b)
        for i in NEAR_ORDER:
            go(gather(b, i))
    drain(keep=14)

    for b in range(2):
        for i in range(7):
            gather(b, i).wait_recv()
        for h in range(2):
            for i in range(SPLIT):
                for block in range(XS):
                    for half in range(CORES):
                        rows = pl.ds(((h * SPLIT + i) * XS + block) * 8, 8)
                        matrix[rows, pl.ds(half * 128, 128)] = core[
                            block, half, h, b * SPLIT + i
                        ]
        chi, clo = halves(matrix[...])
        high, low = halves(nt(dhi[...], chi) + nt(dhi[...], clo) + nt(dlo[...], chi))
        spread[...] = jnp.concatenate([high, low, high], axis=1)
        for j in range(2048 // TILE):
            m = pl.ds(j * TILE, TILE)
            high, low = bhi[b, :, :, m].reshape(128, TILE), blo[b, :, :, m].reshape(128, TILE)
            removed = nn(spread[...], jnp.concatenate([high, high, low], axis=0))
            kept = x_v if b == 0 else out_v
            out_v[:, :, m] = kept[:, :, m] - removed.reshape(4, 64, TILE)
    drain()


def shards(snapshots, space_basis, sample_basis):
    vmem = pltpu.VMEM
    dma = pltpu.SemaphoreType.DMA
    hbm = pl.BlockSpec(memory_space=pltpu.HBM)
    return pl.pallas_call(
        kernel,
        name="deflate",
        out_shape=jax.ShapeDtypeStruct((4, 64, 2048), f32),
        in_specs=[hbm] * 3,
        out_specs=pl.BlockSpec(memory_space=pltpu.VMEM),
        scratch_shapes=[
            vmem((4, 64, 2048), f32),
            vmem((64, 64), f32),
            vmem((2, CHUNKS, XS, 8, 2048), f32),
            vmem((2, 2, SPLIT * 32, 2048), bf16),
            vmem((2, 2, SPLIT * 32, 2048), bf16),
            vmem((256, 2048), bf16),
            vmem((256, 2048), bf16),
            vmem((256, 256), f32),
            vmem((256, 256), bf16),
            vmem((256, 256), bf16),
            vmem((256, 256), bf16),
            vmem((256, 256), bf16),
            vmem((2, CORES, CHUNKS, XS, 8, 128), f32),
            vmem((2, 7, CHUNKS, 8, 128), f32),
            vmem((2, CHUNKS, 8, 128), f32),
            vmem((2, 7, CHUNKS, 8, 128), f32),
            vmem((2, CHUNKS, 8, 128), f32),
            vmem((2, 7, CHUNKS, 8, 128), f32),
            vmem((XS, CORES, 2, CHUNKS, 8, 128), f32),
            vmem((128, 256), f32),
            vmem((256, 384), bf16),
            dma((CHUNKS + 2,)),
            dma((CHUNKS,)), dma((CHUNKS,)),
            dma((2, 2)), dma((2, 2)),
            dma((2,)), dma((2,)),
            dma((CHUNKS, 3)), dma((CHUNKS, 3)),
            dma((2, 2, 7)), dma((2, 2, 7)),
            dma((2, 2, 7)), dma((2, 2, 7)),
            dma((2, 2, 7)), dma((2, 2, 7)),
            dma((2, 7)), dma((2, 7)),
        ],
        compiler_params=pltpu.CompilerParams(
            collective_id=0, has_side_effects=True, vmem_limit_bytes=32 * 2**20
        ),
    )(*(pltpu.with_memory_space_constraint(a, pltpu.HBM) for a in (snapshots, space_basis, sample_basis)))


def solution(mesh):
    return jax.shard_map(
        shards,
        mesh=mesh,
        in_specs=(P(None, "samp", "space"), P("samp", "space"), P("samp", None)),
        out_specs=P(None, "samp", "space"),
        check_vma=False,
    )
```
